256 devices in a mesh: segment: 2 (over y_hi), seq: 128 (over z, x, y_lo, core).
Axes of the slice: x: 4, y: 4 (y_hi: 2, y_lo: 2; y = y_hi * 2 + y_lo), z: 8, core: 2. Of those that a mesh axis runs over, the one named last changes fastest.
Arguments:
- latent: bfloat16 [32768, 5120], P('seq'), may hold values from -6 to 6
- stale_hidden: bfloat16 [32768, 5120], P('seq'), may hold values from -6 to 6
- step_ids: int32 [3], replicated, may hold values from 0 to 999, as said below
- sigma_table: int32 [1000], replicated, may hold values from 1 to 1000, as said below
- mod_weight: bfloat16 [2, 256, 15360], P('segment', None, 'seq'), may hold values from -0.375 to 0.375
Outputs:
- latent_next: bfloat16 [32768, 5120], P('seq')
- hidden_last: bfloat16 [32768, 5120], P('seq')
The draws below stay inside these ranges and needn't reach their ends.
Inputs may be any that keep to these rules, and one draw needn't show every extreme that they name: `step_ids`: strictly falling along the steps. `sigma_table`: never falling along the table.
All inputs are finite; a program needn't handle non-finite values.
Results may differ from the reference program's by a relative error of at most 0.014.
Values may be sent and summed in bfloat16 or wider, within the bound.
A program may use at most 128 MiB of HBM per device.

```python
import math
import jax
import jax.numpy as jnp
from jax import lax

D = 5120
HEADS = 40
FREQ = 256
HEAD = 128
WINDOW = 128
TOK_DEV = 256
STEPS = 2
TABLE = 1000
SEGMENTS = 2
TOKENS = 32768


def draw_step_ids(key, part):
    key = jax.random.fold_in(key, 3)
    first_key, fall_key = jax.random.split(key)
    first = TABLE - 1 - jax.random.randint(first_key, (1,), 0, 100)
    falls = jax.random.randint(fall_key, (STEPS,), 150, 300)
    return jnp.concatenate([first, first - jnp.cumsum(falls)]).astype(jnp.int32)


def draw_sigma_table(key, part):
    key = jax.random.fold_in(key, 5)
    levels = jax.random.randint(key, (TABLE,), 1, 1001)
    return jnp.sort(levels).astype(jnp.int32)


def block_levels(stream_key, dims, cuts, least, largest):
    level = 1.0
    for axis_at, shards_of in cuts:
        heights = jax.random.uniform(jax.random.fold_in(jax.random.fold_in(stream_key, 6), axis_at), (shards_of,), jnp.float32, least / len(cuts), largest / len(cuts))
        level = level * jnp.repeat(jnp.exp(heights), dims[axis_at] // shards_of).reshape((-1,) + (1,) * (len(dims) - 1 - axis_at))
    return level


def gaussian(own_key, extent, spread, bound, shards=(), kind=jnp.bfloat16):
    values = jax.random.normal(own_key, extent, jnp.float32) * spread
    if len(shards) > 0:
        values = block_levels(own_key, extent, shards, -0.22, 0.18) * values
    return jnp.clip(values, min=-bound, max=bound).astype(kind)


def setup_inputs(seed: int = 0) -> dict:
    seeds = jax.random.split(jax.random.key(seed), 6)
    return {
        "latent": gaussian(seeds[0], (TOKENS, D), 1.0, 6.0, ((0, 128),)),
        "stale_hidden": gaussian(seeds[1], (TOKENS, D), 1.0, 6.0, ((0, 128),)),
        "step_ids": draw_step_ids(jax.random.fold_in(seeds[5], 71), 0),
        "sigma_table": draw_sigma_table(jax.random.fold_in(seeds[5], 71), 0),
        "mod_weight": gaussian(seeds[4], (SEGMENTS, FREQ, 3 * D), FREQ ** -0.5, 0.375, ((0, 2), (2, 128))),
    }


def embed(t_value):
    half = FREQ // 2
    freqs = jnp.exp(-math.log(10000.0) * jnp.arange(half, dtype=jnp.float32) / half)
    angles = t_value * freqs
    return jnp.concatenate([jnp.cos(angles), jnp.sin(angles)])

def modulation(t_value, mod_w):
    features = jax.nn.silu(embed(t_value)).astype(jnp.bfloat16)
    return jnp.dot(features, mod_w, preferred_element_type=jnp.float32)

def normalize(hidden, mod):
    shift = mod[:D]
    scale = mod[D:2 * D]
    values = hidden.astype(jnp.float32)
    mean = lax.optimization_barrier(jnp.mean(values, axis=-1, keepdims=True))
    var = lax.optimization_barrier(jnp.mean((values - mean) ** 2, axis=-1, keepdims=True))
    normed = (values - mean) * lax.rsqrt(var + 1e-06)
    return (normed * (1.0 + scale) + shift).astype(jnp.bfloat16)

def attend(query, keys, start, total):
    rows = query.shape[0]
    span = keys.shape[0]
    qpos = start + jnp.arange(rows, dtype=jnp.int32)
    kpos = start - WINDOW + jnp.arange(span, dtype=jnp.int32)
    dist = qpos[:, None] - kpos[None, :]
    allowed = (jnp.abs(dist) <= WINDOW) & (kpos[None, :] >= 0) & (kpos[None, :] < total)
    kfloat = keys.astype(jnp.float32)
    scores = jnp.einsum('qhd,khd->hqk', query.astype(jnp.float32), kfloat) / float(HEAD)
    scores = jnp.where(allowed[None], scores, -jnp.inf)
    top = lax.optimization_barrier(jnp.max(scores, axis=-1, keepdims=True))
    expo = jnp.exp(scores - top)
    probs = (expo / lax.optimization_barrier(jnp.sum(expo, axis=-1, keepdims=True))).astype(jnp.bfloat16)
    out = jnp.einsum('hqk,khd->qhd', probs.astype(jnp.float32), kfloat)
    return out.astype(jnp.bfloat16).reshape(rows, HEADS * HEAD)

def section(hidden, t_value, mod_w):
    mod = modulation(t_value, mod_w)
    normed = normalize(hidden, mod).reshape(TOKENS, HEADS, HEAD)
    padded = jnp.pad(normed, ((WINDOW, WINDOW), (0, 0), (0, 0)))

    def one_block(block):
        start = (block * TOK_DEV).astype(jnp.int32)
        q_rows = lax.dynamic_slice_in_dim(normed, start, TOK_DEV, 0)
        k_rows = lax.dynamic_slice_in_dim(padded, start, TOK_DEV + 2 * WINDOW, 0)
        return attend(q_rows, k_rows, start, TOKENS)
    attn = lax.map(one_block, jnp.arange(TOKENS // TOK_DEV, dtype=jnp.int32)).reshape(TOKENS, D)
    gate = mod[2 * D:]
    return (hidden.astype(jnp.float32) + gate * attn.astype(jnp.float32)).astype(jnp.bfloat16)

def reference(latent, stale_hidden, step_ids, sigma_table, mod_weight):
    state = latent
    hidden = stale_hidden
    for step in range(STEPS):
        t_now = sigma_table[step_ids[step]].astype(jnp.float32)
        t_next = sigma_table[step_ids[step + 1]].astype(jnp.float32)
        fresh = section(state, t_now, mod_weight[0])
        noise = section(hidden, t_now, mod_weight[1])
        state = (state.astype(jnp.float32) + (t_next - t_now) / 1000.0 * noise.astype(jnp.float32)).astype(jnp.bfloat16)
        hidden = fresh
    return (state, hidden)
```

```python
import functools
import math

import jax
import jax.numpy as jnp
from jax import lax
from jax.experimental import pallas as pl
from jax.experimental.pallas import tpu as pltpu
from jax.sharding import PartitionSpec as P

HEADS = 40
HEAD = 128
WINDOW = 128
ROWS = 256
EXT = ROWS + 2 * WINDOW
WIDTH = HEADS * HEAD
PACK = 2
GROUPS = HEADS // PACK
COLS = 120
PLANE = 15
LOG2E = 1.4426950408889634
MASKED = -1e30
MESH = pl.DeviceIdType.MESH
F32 = jnp.float32
BF16 = jnp.bfloat16

LATENT, STALE, FRESH, STATE = range(4)


def features(t_first, t_second, segment):
    shape = (8, HEAD)
    lane = lax.broadcasted_iota(jnp.int32, shape, 1).astype(F32)
    row = lax.broadcasted_iota(jnp.int32, shape, 0)
    freqs = jnp.exp(lane * (-math.log(10000.0) / HEAD))
    angles = jnp.where(row % 2 == 0, t_first, t_second) * freqs
    keep = jnp.where(row // 2 == segment, 1.0, 0.0)
    parts = []
    for value in (jnp.cos(angles), jnp.sin(angles)):
        parts.append(value / (1.0 + jnp.exp(-value)) * keep)
    return jnp.concatenate(parts, axis=1).astype(BF16)


def kernel(
    latent_hbm,
    stale_hbm,
    step_ids,
    sigma_table,
    weight,
    latent_out,
    hidden_out,
    x,
    out,
    rstd,
    offset,
    bias,
    keys,
    msg_out,
    msg_in,
    plane,
    mods,
    load_sem,
    out_sem,
    recv_on,
    recv_off,
    send_on,
    send_off,
    recv_msg,
    send_msg,
    recv_mod1,
    send_mod1,
    recv_mod2,
    send_mod2,
    recv_mod3,
    send_mod3,
):
    seg = lax.axis_index("segment")
    seq = lax.axis_index("seq")
    core = seq % 2
    spot = seq % 4
    across = (seq // 4) % 4
    deep = seq // 16
    quad = seg * 4 + spot
    last = 127
    on_chip = seq + 1 - 2 * core
    off_chip = (seq + 127 + 2 * core) % 128

    src_on = pl.multiple_of(256 - 128 * core, 128)
    src_off = pl.multiple_of(128 + 128 * core, 128)
    dst_on = pl.multiple_of(384 * core, 128)
    dst_off = pl.multiple_of(384 - 384 * core, 128)

    def peer_quad(k):
        other = (quad + k) % 8
        return (other // 4, seq - spot + other % 4)

    def peer_across(k):
        return (seg, seq - across * 4 + (across + k) % 4 * 4)

    def peer_deep(k):
        return (seg, (seq + 16 * k) % 128)

    for arr, source in ((LATENT, latent_hbm), (STALE, stale_hbm)):

        @pl.loop(0, HEADS)
        def _(h, arr=arr, source=source):
            cols = pl.ds(pl.multiple_of(h * HEAD, HEAD), HEAD)
            pltpu.make_async_copy(
                source.at[:, cols], x.at[arr, h, pl.ds(WINDOW, ROWS)], load_sem.at[arr]
            ).start()

    def wait_load(arr):
        whole = x.at[arr, :, pl.ds(WINDOW, ROWS)]
        pltpu.make_async_copy(whole, whole, load_sem.at[arr]).wait()

    barrier = pltpu.get_barrier_semaphore()
    partners = [peer_quad(k) for k in range(1, 8)]
    partners += [peer_across(k) for k in range(1, 4)]
    partners += [peer_deep(k) for k in range(1, 8)]
    partners += [(0, off_chip), (1, off_chip)]
    for partner in partners:
        pl.semaphore_signal(barrier, inc=1, device_id=partner, device_id_type=MESH)

    times = [sigma_table[step_ids[i]].astype(F32) for i in range(3)]
    feats = features(times[0], times[1], seg)
    columns = jnp.dot(feats, weight[0], preferred_element_type=F32)
    plane[across, quad] = jnp.concatenate([columns, jnp.zeros((8, HEAD - COLS), F32)], axis=1)
    rates = [(times[i + 1] - times[i]) * F32(1.0 / 1000.0) for i in range(2)]

    pl.semaphore_wait(barrier, len(partners))

    def mod1(k):
        ref = plane.at[across, quad]
        return pltpu.make_async_remote_copy(
            ref, ref, send_mod1.at[k], recv_mod1.at[k], peer_quad(k), MESH
        )

    def mod2(k):
        ref = plane.at[across]
        return pltpu.make_async_remote_copy(
            ref, ref, send_mod2.at[k], recv_mod2.at[k], peer_across(k), MESH
        )

    def mod3(k):
        ref = mods.at[pl.ds(deep * PLANE, PLANE)]
        return pltpu.make_async_remote_copy(
            ref, ref, send_mod3.at[k], recv_mod3.at[k], peer_deep(k), MESH
        )

    def halo_on(arr, g):
        heads = pl.ds(g * PACK, PACK)
        return pltpu.make_async_remote_copy(
            x.at[arr, heads, pl.ds(src_on, WINDOW)],
            x.at[arr, heads, pl.ds(dst_on, WINDOW)],
            send_on.at[arr],
            recv_on.at[arr, g],
            (seg, on_chip),
            MESH,
        )

    def halo_off(arr, g, to):
        heads = pl.ds(g * PACK, PACK)
        return pltpu.make_async_remote_copy(
            x.at[arr, heads, pl.ds(src_off, WINDOW)],
            x.at[arr, heads, pl.ds(dst_off, WINDOW)],
            send_off.at[arr],
            recv_off.at[arr, g],
            (to, off_chip),
            MESH,
        )

    def send_halo(arr, g):
        halo_on(arr, g).start()

        @pl.when(g % 2 == seg)
        def _():
            halo_off(arr, g, 0).start()
            halo_off(arr, g, 1).start()

    def send_all(arr):
        @pl.loop(0, GROUPS)
        def _(g):
            send_halo(arr, g)

    def message(arr, side):
        return pltpu.make_async_remote_copy(
            msg_out.at[arr, side],
            msg_in.at[arr, side],
            send_msg.at[arr, side],
            recv_msg.at[arr, side],
            (seg, on_chip if side == 0 else off_chip),
            MESH,
        )

    def own_stats(arr):
        own = pl.ds(WINDOW, ROWS)

        def add(h, total):
            return total + x[arr, h, own].astype(F32)

        total = lax.fori_loop(0, HEADS, add, jnp.zeros((ROWS, HEAD), F32))
        mean = jnp.sum(total, axis=1, keepdims=True) * F32(1.0 / WIDTH)
        mean = jnp.broadcast_to(mean, (ROWS, HEAD))
        offset[arr, own] = mean

        def add_square(h, total):
            part = x[arr, h, own].astype(F32) - offset[arr, own]
            return total + part * part

        total = lax.fori_loop(0, HEADS, add_square, jnp.zeros((ROWS, HEAD), F32))
        var = jnp.sum(total, axis=1, keepdims=True) * F32(1.0 / WIDTH)
        scale = jnp.broadcast_to(lax.rsqrt(var + 1e-06), (ROWS, HEAD))
        rstd[arr, own] = scale
        offset[arr, own] = -mean * scale
        row = lax.broadcasted_iota(jnp.int32, (8, HEAD), 0)
        for side, start in ((0, src_on), (1, src_off)):
            first = rstd[arr, pl.ds(start, WINDOW)].T[:8]
            second = offset[arr, pl.ds(start, WINDOW)].T[:8]
            msg_out[arr, side] = jnp.where(row == 0, first, second)
            message(arr, side).start()

    def halo_stats(arr):
        for side, start in ((0, dst_off), (1, dst_on)):
            message(arr, side).wait_recv()
            rows = pl.ds(start, WINDOW)
            got = msg_in[arr, side]
            rstd[arr, rows] = jnp.broadcast_to(got[0:1], (WINDOW, HEAD)).T
            offset[arr, rows] = jnp.broadcast_to(got[1:2], (WINDOW, HEAD)).T

    def rows_of(low):
        return pl.ds(low + WINDOW, WINDOW)

    def run_section(arr, mod_row, finish, after):
        @pl.loop(0, GROUPS)
        def _(g):
            halo_on(arr, g).wait_recv()
            halo_off(arr, g, seg).wait_recv()
            for u in range(PACK):
                h = g * PACK + u
                one_head(arr, mod_row, h, u, finish)
            after(g)

    def one_head(arr, mod_row, h, u, finish):
        shift = mods[h][mod_row : mod_row + 1]
        scale = mods[HEADS + h][mod_row : mod_row + 1] + 1.0
        gate = mods[2 * HEADS + h][mod_row : mod_row + 1]
        raw = x[arr, h].astype(F32)
        normed = (raw * rstd[arr] + offset[arr]) * scale + shift
        keys[u, :, :HEAD] = normed.astype(BF16)
        for b in range(2):
            low = b * WINDOW
            query = keys[u, low + WINDOW : low + 2 * WINDOW, :HEAD]
            span = keys[u, low : low + 3 * WINDOW]
            scores = lax.dot_general(
                query, span[:, :HEAD], (((1,), (1,)), ((), ())), preferred_element_type=F32
            )
            scores = scores * F32(LOG2E / HEAD)
            left = scores[:, :WINDOW] + bias[2 * b]
            mid = scores[:, WINDOW : 2 * WINDOW]
            right = scores[:, 2 * WINDOW :] + bias[2 * b + 1]
            top = jnp.max(jnp.maximum(jnp.maximum(left, right), mid), axis=1, keepdims=True)
            expo = jnp.concatenate(
                [jnp.exp2(part - top).astype(BF16) for part in (left, mid, right)], axis=1
            )
            both = jnp.dot(expo, span, preferred_element_type=F32)
            attn = both[:, :HEAD] / both[:, HEAD:]
            own = x[arr, h, rows_of(low)].astype(F32)
            finish(h, low, own + gate * attn)

    for k in range(1, 8):
        mod1(k).start()
    wait_load(LATENT)
    send_all(LATENT)
    for k in range(1, 8):
        mod1(k).wait_recv()
    for k in range(1, 4):
        mod2(k).start()

    keys[:, :, HEAD:] = jnp.ones((PACK, EXT, HEAD), BF16)
    query_at = lax.broadcasted_iota(jnp.int32, (WINDOW, WINDOW), 0)
    key_at = lax.broadcasted_iota(jnp.int32, (WINDOW, WINDOW), 1)
    left_bias = jnp.where(key_at >= query_at, 0.0, MASKED)
    right_bias = jnp.where(key_at <= query_at, 0.0, MASKED)
    bias[0] = jnp.where(seq == 0, MASKED, left_bias)
    bias[1] = right_bias
    bias[2] = left_bias
    bias[3] = jnp.where(seq == last, MASKED, right_bias)
    own_stats(LATENT)

    for k in range(1, 4):
        mod2(k).wait_recv()
    lane = lax.broadcasted_iota(jnp.int32, (8, HEAD), 1)

    def chunk(k):
        return plane[k // 4, k % 4] + plane[k // 4, 4 + k % 4]

    for k in range(PLANE):
        first, second = chunk(k), chunk(k + 1)
        if k > 0:
            first = pltpu.roll(first, HEAD - 8 * k, 1)
        second = pltpu.roll(second, COLS - 8 * k, 1)
        row = jnp.where(lane < COLS - 8 * k, first, second)
        mods[deep * PLANE + k] = row[:4]
    for k in range(1, 8):
        mod3(k).start()

    wait_load(STALE)
    send_all(STALE)
    own_stats(STALE)
    for k in range(1, 8):
        mod3(k).wait_recv()

    def to_fresh(h, low, value):
        x[FRESH, h, rows_of(low)] = value.astype(BF16)

    def to_state(h, low, value):
        now = x[LATENT, h, rows_of(low)].astype(F32)
        x[STATE, h, rows_of(low)] = (now + rates[0] * value).astype(BF16)

    def to_latent_out(h, low, value):
        now = x[STATE, h, rows_of(low)].astype(F32)
        out[0, h, low : low + WINDOW] = (now + rates[1] * value).astype(BF16)

    def to_hidden_out(h, low, value):
        out[1, h, low : low + WINDOW] = value.astype(BF16)

    def write(which, target):
        def after(g):
            for u in range(PACK):
                h = g * PACK + u
                cols = pl.ds(pl.multiple_of(h * HEAD, HEAD), HEAD)
                pltpu.make_async_copy(out.at[which, h], target.at[:, cols], out_sem.at[which]).start()

        return after

    halo_stats(LATENT)
    run_section(LATENT, 0, to_fresh, functools.partial(send_halo, FRESH))
    own_stats(FRESH)
    halo_stats(STALE)
    run_section(STALE, 2, to_state, functools.partial(send_halo, STATE))
    own_stats(STATE)
    halo_stats(FRESH)
    run_section(FRESH, 3, to_latent_out, write(0, latent_out))
    halo_stats(STATE)
    run_section(STATE, 1, to_hidden_out, write(1, hidden_out))

    for which in range(2):
        pltpu.make_async_copy(out.at[which], out.at[which], out_sem.at[which]).wait()
    for k in range(1, 8):
        mod1(k).wait_send()
        mod3(k).wait_send()
    for k in range(1, 4):
        mod2(k).wait_send()
    for arr in range(4):
        for side in range(2):
            message(arr, side).wait_send()
        sent = x.at[arr, :, pl.ds(0, WINDOW)]
        pltpu.make_async_copy(sent, sent, send_on.at[arr]).wait()
        pltpu.make_async_copy(sent, sent, send_off.at[arr]).wait()


def per_device(latent, stale_hidden, step_ids, sigma_table, mod_weight):
    dma = pltpu.SemaphoreType.DMA
    anywhere = pl.BlockSpec(memory_space=pl.ANY)
    scalars = pl.BlockSpec(memory_space=pltpu.SMEM)
    result = jax.ShapeDtypeStruct(latent.shape, latent.dtype)
    return pl.pallas_call(
        kernel,
        out_shape=(result, result),
        in_specs=[anywhere, anywhere, scalars, scalars, pl.BlockSpec(memory_space=pltpu.VMEM)],
        out_specs=(anywhere, anywhere),
        scratch_shapes=[
            pltpu.VMEM((4, HEADS, EXT, HEAD), BF16),
            pltpu.VMEM((2, HEADS, ROWS, HEAD), BF16),
            pltpu.VMEM((4, EXT, HEAD), F32),
            pltpu.VMEM((4, EXT, HEAD), F32),
            pltpu.VMEM((4, WINDOW, WINDOW), F32),
            pltpu.VMEM((PACK, EXT, 2 * HEAD), BF16),
            pltpu.VMEM((4, 2, 8, HEAD), F32),
            pltpu.VMEM((4, 2, 8, HEAD), F32),
            pltpu.VMEM((4, 8, 8, HEAD), F32),
            pltpu.VMEM((3 * HEADS, 4, HEAD), F32),
            dma((2,)),
            dma((2,)),
            dma((4, GROUPS)),
            dma((4, GROUPS)),
            dma((4,)),
            dma((4,)),
            dma((4, 2)),
            dma((4, 2)),
            dma((8,)),
            dma((8,)),
            dma((4,)),
            dma((4,)),
            dma((8,)),
            dma((8,)),
        ],
        compiler_params=pltpu.CompilerParams(
            collective_id=0, has_side_effects=True, vmem_limit_bytes=48 * 1024 * 1024
        ),
    )(latent, stale_hidden, step_ids, sigma_table, mod_weight)


def solution(mesh):
    placed = (P("seq", None), P("seq", None), P(), P(), P("segment", None, "seq"))
    return jax.shard_map(
        per_device,
        mesh=mesh,
        in_specs=placed,
        out_specs=(P("seq", None), P("seq", None)),
        check_vma=False,
    )
```

```python
import functools
import math

import jax
import jax.numpy as jnp
from jax import lax
from jax.experimental import pallas as pl
from jax.experimental.pallas import tpu as pltpu
from jax.sharding import PartitionSpec as P

HEADS = 40
HEAD = 128
WINDOW = 128
ROWS = 256
EXT = ROWS + 2 * WINDOW
WIDTH = HEADS * HEAD
PACK = 8
GROUPS = HEADS // PACK
COLS = 120
PLANE = 15
ROOT = math.sqrt(math.log2(math.e) / HEAD)
MASKED = -1e30
MESH = pl.DeviceIdType.MESH
F32 = jnp.float32
BF16 = jnp.bfloat16

LATENT, STALE, FRESH, STATE = range(4)


def features(t_first, t_second, segment):
    shape = (8, HEAD)
    lane = lax.broadcasted_iota(jnp.int32, shape, 1).astype(F32)
    row = lax.broadcasted_iota(jnp.int32, shape, 0)
    freqs = jnp.exp(lane * (-math.log(10000.0) / HEAD))
    angles = jnp.where(row % 2 == 0, t_first, t_second) * freqs
    keep = jnp.where(row // 2 == segment, 1.0, 0.0)
    parts = []
    for value in (jnp.cos(angles), jnp.sin(angles)):
        parts.append(value / (1.0 + jnp.exp(-value)) * keep)
    return jnp.concatenate(parts, axis=1).astype(BF16)


def kernel(
    latent_hbm,
    stale_hbm,
    step_ids,
    sigma_table,
    weight,
    latent_out,
    hidden_out,
    x_latent,
    x_stale,
    x_fresh,
    x_state,
    out_latent,
    out_hidden,
    rstd,
    offset,
    bias,
    keys,
    msg_out,
    msg_in,
    plane,
    mods,
    load_sem,
    out_sem,
    recv_on,
    recv_off,
    send_on,
    send_off,
    recv_msg,
    send_msg,
    recv_mod1,
    send_mod1,
    recv_mod2,
    send_mod2,
    recv_mod3,
    send_mod3,
):
    x = (x_latent, x_stale, x_fresh, x_state)
    out = (out_latent, out_hidden)
    seg = lax.axis_index("segment")
    seq = lax.axis_index("seq")
    core = seq % 2
    spot = seq % 4
    across = (seq // 4) % 4
    deep = seq // 16
    quad = seg * 4 + spot
    last = 127
    on_chip = seq + 1 - 2 * core
    off_chip = (seq + 127 + 2 * core) % 128

    src_on = pl.multiple_of(256 - 128 * core, 128)
    src_off = pl.multiple_of(128 + 128 * core, 128)
    dst_on = pl.multiple_of(384 * core, 128)
    dst_off = pl.multiple_of(384 - 384 * core, 128)

    def peer_quad(k):
        other = (quad + k) % 8
        return (other // 4, seq - spot + other % 4)

    def peer_across(k):
        return (seg, seq - across * 4 + (across + k) % 4 * 4)

    def peer_deep(k):
        return (seg, (seq + 16 * k) % 128)

    for arr, source in ((LATENT, latent_hbm), (STALE, stale_hbm)):

        @pl.loop(0, HEADS)
        def _(h, arr=arr, source=source):
            cols = pl.ds(pl.multiple_of(h * HEAD, HEAD), HEAD)
            pltpu.make_async_copy(
                source.at[:, cols], x[arr].at[h, pl.ds(WINDOW, ROWS)], load_sem.at[arr]
            ).start()

    def wait_load(arr):
        whole = x[arr].at[:, pl.ds(WINDOW, ROWS)]
        pltpu.make_async_copy(whole, whole, load_sem.at[arr]).wait()

    barrier = pltpu.get_barrier_semaphore()
    partners = [peer_quad(k) for k in range(1, 8)]
    partners += [peer_across(k) for k in range(1, 4)]
    partners += [peer_deep(k) for k in range(1, 8)]
    partners += [(0, off_chip), (1, off_chip)]
    for partner in partners:
        pl.semaphore_signal(barrier, inc=1, device_id=partner, device_id_type=MESH)

    times = [sigma_table[step_ids[i]].astype(F32) for i in range(3)]
    feats = features(times[0], times[1], seg)
    columns = jnp.dot(feats, weight[0], preferred_element_type=F32)
    plane[across, quad] = jnp.concatenate([columns, jnp.zeros((8, HEAD - COLS), F32)], axis=1)
    rates = [(times[i + 1] - times[i]) * F32(1.0 / 1000.0) for i in range(2)]

    pl.semaphore_wait(barrier, len(partners))

    def mod1(k):
        ref = plane.at[across, quad]
        return pltpu.make_async_remote_copy(
            ref, ref, send_mod1.at[k], recv_mod1.at[k], peer_quad(k), MESH
        )

    def mod2(k):
        ref = plane.at[across]
        return pltpu.make_async_remote_copy(
            ref, ref, send_mod2.at[k], recv_mod2.at[k], peer_across(k), MESH
        )

    def mod3(k):
        ref = mods.at[pl.ds(deep * PLANE, PLANE)]
        return pltpu.make_async_remote_copy(
            ref, ref, send_mod3.at[k], recv_mod3.at[k], peer_deep(k), MESH
        )

    def halo_on(arr, g):
        heads = pl.ds(g * PACK, PACK)
        return pltpu.make_async_remote_copy(
            x[arr].at[heads, pl.ds(src_on, WINDOW)],
            x[arr].at[heads, pl.ds(dst_on, WINDOW)],
            send_on.at[arr],
            recv_on.at[arr, g],
            (seg, on_chip),
            MESH,
        )

    def halo_off(arr, g, half, to):
        heads = pl.ds(g * PACK + half * (PACK // 2), PACK // 2)
        return pltpu.make_async_remote_copy(
            x[arr].at[heads, pl.ds(src_off, WINDOW)],
            x[arr].at[heads, pl.ds(dst_off, WINDOW)],
            send_off.at[arr],
            recv_off.at[arr, 2 * g + half],
            (to, off_chip),
            MESH,
        )

    def send_halo(arr, g):
        halo_on(arr, g).start()
        halo_off(arr, g, seg, 0).start()
        halo_off(arr, g, seg, 1).start()

    def send_all(arr):
        @pl.loop(0, GROUPS)
        def _(g):
            send_halo(arr, g)

    def message(arr, side):
        return pltpu.make_async_remote_copy(
            msg_out.at[arr, side],
            msg_in.at[arr, side],
            send_msg.at[arr, side],
            recv_msg.at[arr, side],
            (seg, on_chip if side == 0 else off_chip),
            MESH,
        )

    def own_stats(arr):
        own = pl.ds(WINDOW, ROWS)

        def add(h, total):
            return total + x[arr][h, own].astype(F32)

        total = lax.fori_loop(0, HEADS, add, jnp.zeros((ROWS, HEAD), F32), unroll=4)
        mean = jnp.sum(total, axis=1, keepdims=True) * F32(1.0 / WIDTH)
        mean = jnp.broadcast_to(mean, (ROWS, HEAD))
        offset[arr, own] = mean

        def add_square(h, total):
            part = x[arr][h, own].astype(F32) - offset[arr, own]
            return total + part * part

        total = lax.fori_loop(0, HEADS, add_square, jnp.zeros((ROWS, HEAD), F32), unroll=4)
        var = jnp.sum(total, axis=1, keepdims=True) * F32(1.0 / WIDTH)
        scale = jnp.broadcast_to(lax.rsqrt(var + 1e-06), (ROWS, HEAD))
        rstd[arr, own] = scale
        offset[arr, own] = -mean * scale
        row = lax.broadcasted_iota(jnp.int32, (8, HEAD), 0)
        for side, start in ((0, src_on), (1, src_off)):
            first = rstd[arr, pl.ds(start, WINDOW)].T[:8]
            second = offset[arr, pl.ds(start, WINDOW)].T[:8]
            msg_out[arr, side] = jnp.where(row == 0, first, second)
            message(arr, side).start()

    def halo_stats(arr):
        for side, start in ((0, dst_off), (1, dst_on)):
            message(arr, side).wait_recv()
            rows = pl.ds(start, WINDOW)
            got = msg_in[arr, side]
            rstd[arr, rows] = jnp.broadcast_to(got[0:1], (WINDOW, HEAD)).T
            offset[arr, rows] = jnp.broadcast_to(got[1:2], (WINDOW, HEAD)).T

    def run_section(arr, mod_row, finish, after):
        @pl.loop(0, GROUPS)
        def _(g):
            halo_on(arr, g).wait_recv()
            halo_off(arr, g, 0, seg).wait_recv()
            halo_off(arr, g, 1, seg).wait_recv()
            heads = [g * PACK + u for u in range(PACK)]
            for u, h in enumerate(heads):
                shift = mods[h][mod_row : mod_row + 1]
                scale = mods[HEADS + h][mod_row : mod_row + 1]
                raw = x[arr][h].astype(F32)
                normed = (raw * rstd[arr] + offset[arr]) * scale + shift
                keys[u, :, :HEAD] = normed.astype(BF16)
            results = []
            for u, h in enumerate(heads):
                gate = mods[2 * HEADS + h][mod_row : mod_row + 1]
                attn = attend(u)
                for b in range(2):
                    own = x[arr][h, rows_of(b)].astype(F32)
                    part = attn[b * WINDOW : (b + 1) * WINDOW]
                    results.append((h, b, own + gate * part))
            finish(results)
            after(g)

    def attend(u):
        scores = lax.dot_general(
            keys[u, WINDOW : WINDOW + ROWS, :HEAD],
            keys[u, :, :HEAD],
            (((1,), (1,)), ((), ())),
            preferred_element_type=F32,
        )
        blocks = []
        none = jnp.zeros((WINDOW, WINDOW), BF16)
        for b in range(2):
            rows = scores[b * WINDOW : (b + 1) * WINDOW, b * WINDOW : (b + 3) * WINDOW]
            left = rows[:, :WINDOW] + bias[2 * b]
            mid = rows[:, WINDOW : 2 * WINDOW]
            right = rows[:, 2 * WINDOW :] + bias[2 * b + 1]
            top = jnp.max(jnp.maximum(jnp.maximum(left, right), mid), axis=1, keepdims=True)
            expo = [jnp.exp2(part - top).astype(BF16) for part in (left, mid, right)]
            blocks.append(jnp.concatenate([none] * b + expo + [none] * (1 - b), axis=1))
        both = jnp.dot(jnp.concatenate(blocks, axis=0), keys[u], preferred_element_type=F32)
        return both[:, :HEAD] * pl.reciprocal(both[:, HEAD:], approx=True)

    def rows_of(b):
        return pl.ds(b * WINDOW + WINDOW, WINDOW)

    for k in range(1, 8):
        mod1(k).start()
    wait_load(LATENT)
    send_all(LATENT)
    for k in range(1, 8):
        mod1(k).wait_recv()
    for k in range(1, 4):
        mod2(k).start()

    keys[:, :, HEAD:] = jnp.ones((PACK, EXT, HEAD), BF16)
    query_at = lax.broadcasted_iota(jnp.int32, (WINDOW, WINDOW), 0)
    key_at = lax.broadcasted_iota(jnp.int32, (WINDOW, WINDOW), 1)
    left_bias = jnp.where(key_at >= query_at, 0.0, MASKED)
    right_bias = jnp.where(key_at <= query_at, 0.0, MASKED)
    bias[0] = jnp.where(seq == 0, MASKED, left_bias)
    bias[1] = right_bias
    bias[2] = left_bias
    bias[3] = jnp.where(seq == last, MASKED, right_bias)
    own_stats(LATENT)

    for k in range(1, 4):
        mod2(k).wait_recv()
    lane = lax.broadcasted_iota(jnp.int32, (8, HEAD), 1)

    def chunk(k):
        return plane[k // 4, k % 4] + plane[k // 4, 4 + k % 4]

    for k in range(PLANE):
        first, second = chunk(k), chunk(k + 1)
        if k > 0:
            first = pltpu.roll(first, HEAD - 8 * k, 1)
        second = pltpu.roll(second, COLS - 8 * k, 1)
        row = jnp.where(lane < COLS - 8 * k, first, second)
        at = deep * PLANE + k
        factor = jnp.where(at < 2 * HEADS, F32(ROOT), F32(1.0 / ROOT))
        row = (row + jnp.where(at // HEADS == 1, F32(1.0), F32(0.0))) * factor
        mods[at] = row[:4]
    for k in range(1, 8):
        mod3(k).start()

    wait_load(STALE)
    send_all(STALE)
    own_stats(STALE)
    for k in range(1, 8):
        mod3(k).wait_recv()

    def to_fresh(results):
        for h, b, value in results:
            x[FRESH][h, rows_of(b)] = value.astype(BF16)

    def to_state(results):
        now = [x[LATENT][h, rows_of(b)].astype(F32) for h, b, _ in results]
        for (h, b, value), base in zip(results, now):
            x[STATE][h, rows_of(b)] = (base + rates[0] * value).astype(BF16)

    def to_latent_out(results):
        now = [x[STATE][h, rows_of(b)].astype(F32) for h, b, _ in results]
        for (h, b, value), base in zip(results, now):
            out[0][h, b * WINDOW : (b + 1) * WINDOW] = (base + rates[1] * value).astype(BF16)

    def to_hidden_out(results):
        for h, b, value in results:
            out[1][h, b * WINDOW : (b + 1) * WINDOW] = value.astype(BF16)

    def write(which, target):
        def after(g):
            for u in range(PACK):
                h = g * PACK + u
                cols = pl.ds(pl.multiple_of(h * HEAD, HEAD), HEAD)
                pltpu.make_async_copy(out[which].at[h], target.at[:, cols], out_sem.at[which]).start()

        return after

    halo_stats(LATENT)
    run_section(LATENT, 0, to_fresh, functools.partial(send_halo, FRESH))
    own_stats(FRESH)
    halo_stats(STALE)
    run_section(STALE, 2, to_state, functools.partial(send_halo, STATE))
    own_stats(STATE)
    halo_stats(FRESH)
    run_section(FRESH, 3, to_latent_out, write(0, latent_out))
    halo_stats(STATE)
    run_section(STATE, 1, to_hidden_out, write(1, hidden_out))

    for which in range(2):
        pltpu.make_async_copy(out[which], out[which], out_sem.at[which]).wait()
    for k in range(1, 8):
        mod1(k).wait_send()
        mod3(k).wait_send()
    for k in range(1, 4):
        mod2(k).wait_send()
    for arr in range(4):
        for side in range(2):
            message(arr, side).wait_send()
        sent = x[arr].at[:, pl.ds(0, WINDOW)]
        pltpu.make_async_copy(sent, sent, send_on.at[arr]).wait()
        pltpu.make_async_copy(sent, sent, send_off.at[arr]).wait()


def per_device(latent, stale_hidden, step_ids, sigma_table, mod_weight):
    dma = pltpu.SemaphoreType.DMA
    anywhere = pl.BlockSpec(memory_space=pl.ANY)
    scalars = pl.BlockSpec(memory_space=pltpu.SMEM)
    result = jax.ShapeDtypeStruct(latent.shape, latent.dtype)
    return pl.pallas_call(
        kernel,
        out_shape=(result, result),
        in_specs=[anywhere, anywhere, scalars, scalars, pl.BlockSpec(memory_space=pltpu.VMEM)],
        out_specs=(anywhere, anywhere),
        scratch_shapes=[
            *[pltpu.VMEM((HEADS, EXT, HEAD), BF16)] * 4,
            *[pltpu.VMEM((HEADS, ROWS, HEAD), BF16)] * 2,
            pltpu.VMEM((4, EXT, HEAD), F32),
            pltpu.VMEM((4, EXT, HEAD), F32),
            pltpu.VMEM((4, WINDOW, WINDOW), F32),
            pltpu.VMEM((PACK, EXT, 2 * HEAD), BF16),
            pltpu.VMEM((4, 2, 8, HEAD), F32),
            pltpu.VMEM((4, 2, 8, HEAD), F32),
            pltpu.VMEM((4, 8, 8, HEAD), F32),
            pltpu.VMEM((3 * HEADS, 4, HEAD), F32),
            dma((2,)),
            dma((2,)),
            dma((4, GROUPS)),
            dma((4, 2 * GROUPS)),
            dma((4,)),
            dma((4,)),
            dma((4, 2)),
            dma((4, 2)),
            dma((8,)),
            dma((8,)),
            dma((4,)),
            dma((4,)),
            dma((8,)),
            dma((8,)),
        ],
        compiler_params=pltpu.CompilerParams(
            collective_id=0, has_side_effects=True, vmem_limit_bytes=48 * 1024 * 1024
        ),
    )(latent, stale_hidden, step_ids, sigma_table, mod_weight)


def solution(mesh):
    placed = (P("seq", None), P("seq", None), P(), P(), P("segment", None, "seq"))
    return jax.shard_map(
        per_device,
        mesh=mesh,
        in_specs=placed,
        out_specs=(P("seq", None), P("seq", None)),
        check_vma=False,
    )
```

```python
import math

import jax
import jax.numpy as jnp
from jax import lax
from jax.experimental import pallas as pl
from jax.experimental.pallas import tpu as pltpu
from jax.sharding import PartitionSpec as P

HEADS = 40
HEAD = 128
WINDOW = 128
ROWS = 256
EXT = ROWS + 2 * WINDOW
WIDTH = HEADS * HEAD
PACK = 8
GROUPS = HEADS // PACK
COLS = 120
PLANE = 15
EARLY = 2
ROOT = math.sqrt(math.log2(math.e) / HEAD)
MASKED = -1e30
MESH = pl.DeviceIdType.MESH
F32 = jnp.float32
BF16 = jnp.bfloat16

LATENT, STALE, FRESH, STATE = range(4)


def features(t_first, t_second, segment):
    shape = (8, HEAD)
    lane = lax.broadcasted_iota(jnp.int32, shape, 1).astype(F32)
    row = lax.broadcasted_iota(jnp.int32, shape, 0)
    freqs = jnp.exp(lane * (-math.log(10000.0) / HEAD))
    angles = jnp.where(row % 2 == 0, t_first, t_second) * freqs
    keep = jnp.where(row // 2 == segment, 1.0, 0.0)
    parts = []
    for value in (jnp.cos(angles), jnp.sin(angles)):
        parts.append(value / (1.0 + jnp.exp(-value)) * keep)
    return jnp.concatenate(parts, axis=1).astype(BF16)


def kernel(
    latent_hbm,
    stale_hbm,
    step_ids,
    sigma_table,
    weight,
    latent_out,
    hidden_out,
    x_latent,
    x_stale,
    x_fresh,
    x_state,
    out_latent,
    out_hidden,
    rstd,
    offset,
    bias,
    keys,
    msg_out,
    msg_in,
    plane,
    joint,
    mods,
    load_sem,
    out_sem,
    recv_on,
    recv_off,
    send_on,
    send_off,
    recv_msg,
    send_msg,
    recv_mod1,
    send_mod1,
    recv_mod2,
    send_mod2,
    recv_mod3,
    send_mod3,
    from_below,
    from_above,
):
    x = (x_latent, x_stale, x_fresh, x_state)
    out = (out_latent, out_hidden)
    seg = lax.axis_index("segment")
    seq = lax.axis_index("seq")
    core = seq % 2
    spot = seq % 4
    across = (seq // 4) % 4
    deep = seq // 16
    quad = seg * 4 + spot
    last = 127
    on_chip = seq + 1 - 2 * core
    off_chip = (seq + 127 + 2 * core) % 128

    src_on = pl.multiple_of(256 - 128 * core, 128)
    src_off = pl.multiple_of(128 + 128 * core, 128)
    dst_on = pl.multiple_of(384 * core, 128)
    dst_off = pl.multiple_of(384 - 384 * core, 128)

    def peer_quad(k):
        other = (quad + k) % 8
        return (other // 4, seq - spot + other % 4)

    def peer_across(k):
        return (seg, seq - across * 4 + (across + k) % 4 * 4)

    def peer_deep(k):
        return (seg, (seq + 16 * k) % 128)

    def load(arr, source):
        @pl.loop(0, HEADS)
        def _(h):
            cols = pl.ds(pl.multiple_of(h * HEAD, HEAD), HEAD)
            pltpu.make_async_copy(
                source.at[:, cols], x[arr].at[h, pl.ds(WINDOW, ROWS)], load_sem.at[arr]
            ).start()

    def wait_load(arr):
        whole = x[arr].at[:, pl.ds(WINDOW, ROWS)]
        pltpu.make_async_copy(whole, whole, load_sem.at[arr]).wait()

    inner = (seq > 0) & (seq < last)
    above, below = peer_deep(1), peer_deep(7)
    barrier = pltpu.get_barrier_semaphore()

    @pl.when(inner)
    def _():
        for to in range(2):
            pl.semaphore_signal(barrier, inc=1, device_id=(to, off_chip), device_id_type=MESH)

    partners = [peer_quad(k) for k in range(1, 8)]
    partners += [peer_across(k) for k in range(1, 4)]
    partners += [above, below]
    for partner in partners:
        pl.semaphore_signal(barrier, inc=1, device_id=partner, device_id_type=MESH)
    load(LATENT, latent_hbm)

    times = [sigma_table[step_ids[i]].astype(F32) for i in range(3)]
    feats = features(times[0], times[1], seg)
    columns = lax.dot_general(
        feats, weight[0], (((1,), (1,)), ((), ())), preferred_element_type=F32
    )
    plane[quad] = jnp.concatenate([columns, jnp.zeros((8, HEAD - COLS), F32)], axis=1)
    rates = [(times[i + 1] - times[i]) * F32(1.0 / 1000.0) for i in range(2)]

    @pl.when(inner)
    def _():
        pl.semaphore_wait(barrier, len(partners) + 2)

    @pl.when(jnp.logical_not(inner))
    def _():
        pl.semaphore_wait(barrier, len(partners))

    def tell(up, down):
        if up:
            pl.semaphore_signal(from_below, inc=1, device_id=above, device_id_type=MESH)
        if down:
            pl.semaphore_signal(from_above, inc=1, device_id=below, device_id_type=MESH)

    def mod1(k):
        ref = plane.at[quad]
        return pltpu.make_async_remote_copy(
            ref, ref, send_mod1.at[k], recv_mod1.at[k], peer_quad(k), MESH
        )

    def mod2(k):
        ref = joint.at[across]
        return pltpu.make_async_remote_copy(
            ref, ref, send_mod2.at[k], recv_mod2.at[k], peer_across(k), MESH
        )

    def mod3(k):
        ref = mods.at[pl.ds(deep * PLANE, PLANE)]
        return pltpu.make_async_remote_copy(
            ref, ref, send_mod3.at[k], recv_mod3.at[k], peer_deep(k), MESH
        )

    def halo_on(arr, g):
        heads = pl.ds(g * PACK, PACK)
        return pltpu.make_async_remote_copy(
            x[arr].at[heads, pl.ds(src_on, WINDOW)],
            x[arr].at[heads, pl.ds(dst_on, WINDOW)],
            send_on.at[arr],
            recv_on.at[arr, g],
            (seg, on_chip),
            MESH,
        )

    def halo_off(arr, g, half, to):
        heads = pl.ds(g * PACK + half * (PACK // 2), PACK // 2)
        return pltpu.make_async_remote_copy(
            x[arr].at[heads, pl.ds(src_off, WINDOW)],
            x[arr].at[heads, pl.ds(dst_off, WINDOW)],
            send_off.at[arr],
            recv_off.at[arr, 2 * g + half],
            (to, off_chip),
            MESH,
        )

    def send_halo(arr, g):
        halo_on(arr, g).start()

        @pl.when(inner)
        def _():
            halo_off(arr, g, seg, 0).start()
            halo_off(arr, g, seg, 1).start()

    def send_groups(arr, first, end):
        @pl.loop(first, end)
        def _(g):
            send_halo(arr, g)

    def message(arr, side):
        return pltpu.make_async_remote_copy(
            msg_out.at[arr, side],
            msg_in.at[arr, side],
            send_msg.at[arr, side],
            recv_msg.at[arr, side],
            (seg, on_chip if side == 0 else off_chip),
            MESH,
        )

    def each_side(side, act):
        if side == 0:
            act()
        else:
            pl.when(inner)(act)

    def own_stats(arr):
        own = pl.ds(WINDOW, ROWS)

        def add(h, total):
            return total + x[arr][h, own].astype(F32)

        total = lax.fori_loop(0, HEADS, add, jnp.zeros((ROWS, HEAD), F32), unroll=4)
        mean = jnp.sum(total, axis=1, keepdims=True) * F32(1.0 / WIDTH)
        mean = jnp.broadcast_to(mean, (ROWS, HEAD))
        offset[arr, own] = mean

        def add_square(h, total):
            part = x[arr][h, own].astype(F32) - offset[arr, own]
            return total + part * part

        total = lax.fori_loop(0, HEADS, add_square, jnp.zeros((ROWS, HEAD), F32), unroll=4)
        var = jnp.sum(total, axis=1, keepdims=True) * F32(1.0 / WIDTH)
        scale = jnp.broadcast_to(lax.rsqrt(var + 1e-06), (ROWS, HEAD))
        rstd[arr, own] = scale
        offset[arr, own] = -mean * scale
        row = lax.broadcasted_iota(jnp.int32, (8, HEAD), 0)
        for side, start in ((0, src_on), (1, src_off)):
            first = rstd[arr, pl.ds(start, WINDOW)].T[:8]
            second = offset[arr, pl.ds(start, WINDOW)].T[:8]
            msg_out[arr, side] = jnp.where(row == 0, first, second)
            each_side(side, lambda side=side: message(arr, side).start())

    def halo_stats(arr):
        for side, start in ((0, dst_off), (1, dst_on)):
            each_side(side, lambda side=side: message(arr, side).wait_recv())
            rows = pl.ds(start, WINDOW)
            got = msg_in[arr, side]
            rstd[arr, rows] = jnp.broadcast_to(got[0:1], (WINDOW, HEAD)).T
            offset[arr, rows] = jnp.broadcast_to(got[1:2], (WINDOW, HEAD)).T

    def run_section(arr, mod_row, finish, after):
        @pl.loop(0, GROUPS)
        def _(g):
            halo_on(arr, g).wait_recv()

            @pl.when(inner)
            def _():
                halo_off(arr, g, 0, seg).wait_recv()
                halo_off(arr, g, 1, seg).wait_recv()

            heads = [g * PACK + u for u in range(PACK)]
            for u, h in enumerate(heads):
                shift = mods[h][mod_row : mod_row + 1]
                scale = mods[HEADS + h][mod_row : mod_row + 1]
                raw = x[arr][h].astype(F32)
                normed = (raw * rstd[arr] + offset[arr]) * scale + shift
                keys[u, :, :HEAD] = normed.astype(BF16)
            results = []
            scores, expo = {}, {}
            for step in range(PACK + 2):
                if step < PACK:
                    scores[step] = products(step)
                if 1 <= step <= PACK:
                    expo[step - 1] = weights(scores.pop(step - 1))
                if step >= 2:
                    u = step - 2
                    h = heads[u]
                    gate = mods[2 * HEADS + h][mod_row : mod_row + 1]
                    attn = mixed(u, expo.pop(u))
                    for b in range(2):
                        own = x[arr][h, rows_of(b)].astype(F32)
                        part = attn[b * WINDOW : (b + 1) * WINDOW]
                        results.append((h, b, own + gate * part))
            finish(results)
            after(g)

    def products(u):
        return lax.dot_general(
            keys[u, WINDOW : WINDOW + ROWS, :HEAD],
            keys[u, :, :HEAD],
            (((1,), (1,)), ((), ())),
            preferred_element_type=F32,
        )

    def weights(scores):
        blocks = []
        none = jnp.zeros((WINDOW, WINDOW), BF16)
        for b in range(2):
            rows = scores[b * WINDOW : (b + 1) * WINDOW, b * WINDOW : (b + 3) * WINDOW]
            left = rows[:, :WINDOW] + bias[2 * b]
            mid = rows[:, WINDOW : 2 * WINDOW]
            right = rows[:, 2 * WINDOW :] + bias[2 * b + 1]
            top = jnp.max(jnp.maximum(jnp.maximum(left, right), mid), axis=1, keepdims=True)
            expo = [jnp.exp2(part - top).astype(BF16) for part in (left, mid, right)]
            blocks.append(jnp.concatenate([none] * b + expo + [none] * (1 - b), axis=1))
        return jnp.concatenate(blocks, axis=0)

    def mixed(u, expo):
        both = jnp.dot(expo, keys[u], preferred_element_type=F32)
        return both[:, :HEAD] * pl.reciprocal(both[:, HEAD:], approx=True)

    def rows_of(b):
        return pl.ds(b * WINDOW + WINDOW, WINDOW)

    for k in range(1, 8):
        mod1(k).start()
    tell(True, True)
    wait_load(LATENT)
    send_groups(LATENT, 0, 2)
    load(STALE, stale_hbm)
    keys[:, :, HEAD:] = jnp.ones((PACK, EXT, HEAD), BF16)
    query_at = lax.broadcasted_iota(jnp.int32, (WINDOW, WINDOW), 0)
    key_at = lax.broadcasted_iota(jnp.int32, (WINDOW, WINDOW), 1)
    left_bias = jnp.where(key_at >= query_at, 0.0, MASKED)
    right_bias = jnp.where(key_at <= query_at, 0.0, MASKED)
    bias[0] = jnp.where(seq == 0, MASKED, left_bias)
    bias[1] = right_bias
    bias[2] = left_bias
    bias[3] = jnp.where(seq == last, MASKED, right_bias)

    @pl.when(jnp.logical_not(inner))
    def _():
        none = pl.ds(dst_on, WINDOW)
        for arr in range(4):
            msg_in[arr, 1] = jnp.zeros((8, HEAD), F32)

            @pl.loop(0, HEADS)
            def _(h, arr=arr):
                x[arr][h, none] = jnp.zeros((WINDOW, HEAD), BF16)

    own_stats(LATENT)
    pl.semaphore_wait(from_below, 1)
    pl.semaphore_wait(from_above, 1)
    tell(True, True)
    for k in range(1, 8):
        mod1(k).wait_recv()
    joint[across] = (plane[:4] + plane[4:])[:, :4]
    for k in range(1, 4):
        mod2(k).start()
    send_groups(LATENT, 2, 4)
    wait_load(STALE)
    pl.semaphore_wait(from_below, 1)
    pl.semaphore_wait(from_above, 1)
    tell(True, False)
    own_stats(STALE)

    for k in range(1, 4):
        mod2(k).wait_recv()
    lane = lax.broadcasted_iota(jnp.int32, (8, HEAD), 1)

    def chunk(k):
        return jnp.concatenate([joint[k // 4, k % 4], jnp.zeros((4, HEAD), F32)], axis=0)

    for k in range(PLANE):
        first, second = chunk(k), chunk(k + 1)
        if k > 0:
            first = pltpu.roll(first, HEAD - 8 * k, 1)
        second = pltpu.roll(second, COLS - 8 * k, 1)
        row = jnp.where(lane < COLS - 8 * k, first, second)
        at = deep * PLANE + k
        factor = jnp.where(at < 2 * HEADS, F32(ROOT), F32(1.0 / ROOT))
        row = (row + jnp.where(at // HEADS == 1, F32(1.0), F32(0.0))) * factor
        mods[at] = row[:4]
    pl.semaphore_wait(from_below, 1)
    for k in range(1, 8):
        mod3(k).start()

    send_groups(LATENT, 4, GROUPS)
    send_groups(STALE, 0, GROUPS)
    for k in range(1, 8):
        mod3(k).wait_recv()

    def to_fresh(results):
        for h, b, value in results:
            x[FRESH][h, rows_of(b)] = value.astype(BF16)

    def to_state(results):
        now = [x[LATENT][h, rows_of(b)].astype(F32) for h, b, _ in results]
        for (h, b, value), base in zip(results, now):
            x[STATE][h, rows_of(b)] = (base + rates[0] * value).astype(BF16)

    def to_latent_out(results):
        now = [x[STATE][h, rows_of(b)].astype(F32) for h, b, _ in results]
        for (h, b, value), base in zip(results, now):
            out[0][h, b * WINDOW : (b + 1) * WINDOW] = (base + rates[1] * value).astype(BF16)

    def to_hidden_out(results):
        for h, b, value in results:
            out[1][h, b * WINDOW : (b + 1) * WINDOW] = value.astype(BF16)

    def write(which, target):
        def after(g):
            for u in range(PACK):
                h = g * PACK + u
                cols = pl.ds(pl.multiple_of(h * HEAD, HEAD), HEAD)
                pltpu.make_async_copy(out[which].at[h], target.at[:, cols], out_sem.at[which]).start()

        return after

    def early(g):
        @pl.when(g < EARLY)
        def _():
            send_halo(FRESH, g)

    halo_stats(LATENT)
    run_section(LATENT, 0, to_fresh, early)
    own_stats(FRESH)
    send_groups(FRESH, EARLY, GROUPS)
    halo_stats(STALE)
    run_section(STALE, 2, to_state, lambda g: None)
    own_stats(STATE)
    send_groups(STATE, 0, GROUPS)
    halo_stats(FRESH)
    run_section(FRESH, 3, to_latent_out, write(0, latent_out))
    halo_stats(STATE)
    run_section(STATE, 1, to_hidden_out, write(1, hidden_out))

    for which in range(2):
        pltpu.make_async_copy(out[which], out[which], out_sem.at[which]).wait()
    for k in range(1, 8):
        mod1(k).wait_send()
        mod3(k).wait_send()
    for k in range(1, 4):
        mod2(k).wait_send()
    for arr in range(4):
        for side in range(2):
            each_side(side, lambda side=side, arr=arr: message(arr, side).wait_send())
        sent = x[arr].at[:, pl.ds(0, WINDOW)]
        pltpu.make_async_copy(sent, sent, send_on.at[arr]).wait()

        @pl.when(inner)
        def _(arr=arr, sent=sent):
            pltpu.make_async_copy(sent, sent, send_off.at[arr]).wait()


def per_device(latent, stale_hidden, step_ids, sigma_table, mod_weight):
    dma = pltpu.SemaphoreType.DMA
    anywhere = pl.BlockSpec(memory_space=pl.ANY)
    scalars = pl.BlockSpec(memory_space=pltpu.SMEM)
    result = jax.ShapeDtypeStruct(latent.shape, latent.dtype)
    return pl.pallas_call(
        kernel,
        out_shape=(result, result),
        in_specs=[anywhere, anywhere, scalars, scalars, pl.BlockSpec(memory_space=pltpu.VMEM)],
        out_specs=(anywhere, anywhere),
        scratch_shapes=[
            *[pltpu.VMEM((HEADS, EXT, HEAD), BF16)] * 4,
            *[pltpu.VMEM((HEADS, ROWS, HEAD), BF16)] * 2,
            pltpu.VMEM((4, EXT, HEAD), F32),
            pltpu.VMEM((4, EXT, HEAD), F32),
            pltpu.VMEM((4, WINDOW, WINDOW), F32),
            pltpu.VMEM((PACK, EXT, 2 * HEAD), BF16),
            pltpu.VMEM((4, 2, 8, HEAD), F32),
            pltpu.VMEM((4, 2, 8, HEAD), F32),
            pltpu.VMEM((8, 8, HEAD), F32),
            pltpu.VMEM((4, 4, 4, HEAD), F32),
            pltpu.VMEM((3 * HEADS, 4, HEAD), F32),
            dma((2,)),
            dma((2,)),
            dma((4, GROUPS)),
            dma((4, 2 * GROUPS)),
            dma((4,)),
            dma((4,)),
            dma((4, 2)),
            dma((4, 2)),
            dma((8,)),
            dma((8,)),
            dma((4,)),
            dma((4,)),
            dma((8,)),
            dma((8,)),
            pltpu.SemaphoreType.REGULAR,
            pltpu.SemaphoreType.REGULAR,
        ],
        compiler_params=pltpu.CompilerParams(
            collective_id=0, has_side_effects=True, vmem_limit_bytes=48 * 1024 * 1024
        ),
    )(latent, stale_hidden, step_ids, sigma_table, jnp.swapaxes(mod_weight, 1, 2))


def solution(mesh):
    placed = (P("seq", None), P("seq", None), P(), P(), P("segment", None, "seq"))
    return jax.shard_map(
        per_device,
        mesh=mesh,
        in_specs=placed,
        out_specs=(P("seq", None), P("seq", None)),
        check_vma=False,
    )
```

```python
import math

import jax
import jax.numpy as jnp
from jax import lax
from jax.experimental import pallas as pl
from jax.experimental.pallas import tpu as pltpu
from jax.sharding import PartitionSpec as P

HEADS = 40
HEAD = 128
WINDOW = 128
ROWS = 256
EXT = ROWS + 2 * WINDOW
WIDTH = HEADS * HEAD
PACK = 8
GROUPS = HEADS // PACK
COLS = 120
PLANE = 15
EARLY = 2
ROOT = math.sqrt(math.log2(math.e) / HEAD)
MASKED = -1e30
MESH = pl.DeviceIdType.MESH
F32 = jnp.float32
BF16 = jnp.bfloat16

LATENT, STALE, FRESH, STATE = range(4)


def features(t_first, t_second, segment):
    shape = (8, HEAD)
    lane = lax.broadcasted_iota(jnp.int32, shape, 1).astype(F32)
    row = lax.broadcasted_iota(jnp.int32, shape, 0)
    freqs = jnp.exp(lane * (-math.log(10000.0) / HEAD))
    angles = jnp.where(row % 2 == 0, t_first, t_second) * freqs
    keep = jnp.where(row // 2 == segment, 1.0, 0.0)
    parts = []
    for value in (jnp.cos(angles), jnp.sin(angles)):
        parts.append(value / (1.0 + jnp.exp(-value)) * keep)
    return jnp.concatenate(parts, axis=1).astype(BF16)


def kernel(
    latent_hbm,
    stale_hbm,
    step_ids_hbm,
    sigma_hbm,
    weight_hbm,
    latent_out,
    hidden_out,
    x_latent,
    x_stale,
    x_fresh,
    x_state,
    out_latent,
    out_hidden,
    rstd,
    offset,
    bias,
    keys,
    msg_out,
    msg_in,
    plane,
    joint,
    mods,
    load_sem,
    out_sem,
    recv_on,
    recv_off,
    send_on,
    send_off,
    recv_msg,
    send_msg,
    recv_mod1,
    send_mod1,
    recv_mod2,
    send_mod2,
    recv_mod3,
    send_mod3,
    from_below,
    from_above,
    step_ids,
    sigma_table,
    weight,
    small_sem,
):
    x = (x_latent, x_stale, x_fresh, x_state)
    out = (out_latent, out_hidden)
    seg = lax.axis_index("segment")
    seq = lax.axis_index("seq")
    core = seq % 2
    spot = seq % 4
    across = (seq // 4) % 4
    deep = seq // 16
    quad = seg * 4 + spot
    last = 127
    on_chip = seq + 1 - 2 * core
    off_chip = (seq + 127 + 2 * core) % 128

    src_on = pl.multiple_of(256 - 128 * core, 128)
    src_off = pl.multiple_of(128 + 128 * core, 128)
    dst_on = pl.multiple_of(384 * core, 128)
    dst_off = pl.multiple_of(384 - 384 * core, 128)

    def peer_quad(k):
        other = (quad + k) % 8
        return (other // 4, seq - spot + other % 4)

    def peer_across(k):
        return (seg, seq - across * 4 + (across + k) % 4 * 4)

    def peer_deep(k):
        return (seg, (seq + 16 * k) % 128)

    def load(arr, source):
        @pl.loop(0, HEADS)
        def _(h):
            cols = pl.ds(pl.multiple_of(h * HEAD, HEAD), HEAD)
            pltpu.make_async_copy(
                source.at[:, cols], x[arr].at[h, pl.ds(WINDOW, ROWS)], load_sem.at[arr]
            ).start()

    def wait_load(arr):
        whole = x[arr].at[:, pl.ds(WINDOW, ROWS)]
        pltpu.make_async_copy(whole, whole, load_sem.at[arr]).wait()

    small = [
        pltpu.make_async_copy(source, target, small_sem.at[i])
        for i, (source, target) in enumerate(
            ((step_ids_hbm, step_ids), (sigma_hbm, sigma_table), (weight_hbm, weight))
        )
    ]
    for copy in small:
        copy.start()

    inner = (seq > 0) & (seq < last)
    above, below = peer_deep(1), peer_deep(7)
    barrier = pltpu.get_barrier_semaphore()

    @pl.when(inner)
    def _():
        for to in range(2):
            pl.semaphore_signal(barrier, inc=1, device_id=(to, off_chip), device_id_type=MESH)

    partners = [peer_quad(k) for k in range(1, 8)]
    partners += [peer_across(k) for k in range(1, 4)]
    partners += [above, below]
    for partner in partners:
        pl.semaphore_signal(barrier, inc=1, device_id=partner, device_id_type=MESH)
    load(LATENT, latent_hbm)

    for copy in small:
        copy.wait()
    times = [sigma_table[step_ids[i]].astype(F32) for i in range(3)]
    feats = features(times[0], times[1], seg)
    columns = lax.dot_general(
        feats, weight[0], (((1,), (1,)), ((), ())), preferred_element_type=F32
    )
    plane[quad] = jnp.concatenate([columns, jnp.zeros((8, HEAD - COLS), F32)], axis=1)
    rates = [(times[i + 1] - times[i]) * F32(1.0 / 1000.0) for i in range(2)]

    @pl.when(inner)
    def _():
        pl.semaphore_wait(barrier, len(partners) + 2)

    @pl.when(jnp.logical_not(inner))
    def _():
        pl.semaphore_wait(barrier, len(partners))

    def tell(up, down):
        if up:
            pl.semaphore_signal(from_below, inc=1, device_id=above, device_id_type=MESH)
        if down:
            pl.semaphore_signal(from_above, inc=1, device_id=below, device_id_type=MESH)

    def mod1(k):
        ref = plane.at[quad]
        return pltpu.make_async_remote_copy(
            ref, ref, send_mod1.at[k], recv_mod1.at[k], peer_quad(k), MESH
        )

    def mod2(k):
        ref = joint.at[across]
        return pltpu.make_async_remote_copy(
            ref, ref, send_mod2.at[k], recv_mod2.at[k], peer_across(k), MESH
        )

    def mod3(k):
        ref = mods.at[pl.ds(deep * PLANE, PLANE)]
        return pltpu.make_async_remote_copy(
            ref, ref, send_mod3.at[k], recv_mod3.at[k], peer_deep(k), MESH
        )

    def halo_on(arr, g):
        heads = pl.ds(g * PACK, PACK)
        return pltpu.make_async_remote_copy(
            x[arr].at[heads, pl.ds(src_on, WINDOW)],
            x[arr].at[heads, pl.ds(dst_on, WINDOW)],
            send_on.at[arr],
            recv_on.at[arr, g],
            (seg, on_chip),
            MESH,
        )

    def halo_off(arr, g, half, to):
        heads = pl.ds(g * PACK + half * (PACK // 2), PACK // 2)
        return pltpu.make_async_remote_copy(
            x[arr].at[heads, pl.ds(src_off, WINDOW)],
            x[arr].at[heads, pl.ds(dst_off, WINDOW)],
            send_off.at[arr],
            recv_off.at[arr, 2 * g + half],
            (to, off_chip),
            MESH,
        )

    def send_halo(arr, g):
        halo_on(arr, g).start()

        @pl.when(inner)
        def _():
            halo_off(arr, g, seg, 0).start()
            halo_off(arr, g, seg, 1).start()

    def send_groups(arr, first, end):
        @pl.loop(first, end)
        def _(g):
            send_halo(arr, g)

    def message(arr, side):
        return pltpu.make_async_remote_copy(
            msg_out.at[arr, side],
            msg_in.at[arr, side],
            send_msg.at[arr, side],
            recv_msg.at[arr, side],
            (seg, on_chip if side == 0 else off_chip),
            MESH,
        )

    def each_side(side, act):
        if side == 0:
            act()
        else:
            pl.when(inner)(act)

    def own_stats(arr):
        own = pl.ds(WINDOW, ROWS)

        def add(h, total):
            return total + x[arr][h, own].astype(F32)

        total = lax.fori_loop(0, HEADS, add, jnp.zeros((ROWS, HEAD), F32), unroll=4)
        mean = jnp.sum(total, axis=1, keepdims=True) * F32(1.0 / WIDTH)
        mean = jnp.broadcast_to(mean, (ROWS, HEAD))
        offset[arr, own] = mean

        def add_square(h, total):
            part = x[arr][h, own].astype(F32) - offset[arr, own]
            return total + part * part

        total = lax.fori_loop(0, HEADS, add_square, jnp.zeros((ROWS, HEAD), F32), unroll=4)
        var = jnp.sum(total, axis=1, keepdims=True) * F32(1.0 / WIDTH)
        scale = jnp.broadcast_to(lax.rsqrt(var + 1e-06), (ROWS, HEAD))
        rstd[arr, own] = scale
        offset[arr, own] = -mean * scale
        row = lax.broadcasted_iota(jnp.int32, (8, HEAD), 0)
        for side, start in ((0, src_on), (1, src_off)):
            first = rstd[arr, pl.ds(start, WINDOW)].T[:8]
            second = offset[arr, pl.ds(start, WINDOW)].T[:8]
            msg_out[arr, side] = jnp.where(row == 0, first, second)
            each_side(side, lambda side=side: message(arr, side).start())

    def halo_stats(arr):
        for side, start in ((0, dst_off), (1, dst_on)):
            each_side(side, lambda side=side: message(arr, side).wait_recv())
            rows = pl.ds(start, WINDOW)
            got = msg_in[arr, side]
            rstd[arr, rows] = jnp.broadcast_to(got[0:1], (WINDOW, HEAD)).T
            offset[arr, rows] = jnp.broadcast_to(got[1:2], (WINDOW, HEAD)).T

    def run_section(arr, mod_row, finish, after):
        @pl.loop(0, GROUPS)
        def _(g):
            halo_on(arr, g).wait_recv()

            @pl.when(inner)
            def _():
                halo_off(arr, g, 0, seg).wait_recv()
                halo_off(arr, g, 1, seg).wait_recv()

            heads = [g * PACK + u for u in range(PACK)]
            for u, h in enumerate(heads):
                shift = mods[h][mod_row : mod_row + 1]
                scale = mods[HEADS + h][mod_row : mod_row + 1]
                raw = x[arr][h].astype(F32)
                normed = (raw * rstd[arr] + offset[arr]) * scale + shift
                keys[u, :, :HEAD] = normed.astype(BF16)
            results = []
            scores, expo = {}, {}
            for step in range(PACK + 2):
                if step < PACK:
                    scores[step] = products(step)
                if 1 <= step <= PACK:
                    expo[step - 1] = weights(scores.pop(step - 1))
                if step >= 2:
                    u = step - 2
                    h = heads[u]
                    gate = mods[2 * HEADS + h][mod_row : mod_row + 1]
                    attn = mixed(u, expo.pop(u))
                    for b in range(2):
                        own = x[arr][h, rows_of(b)].astype(F32)
                        part = attn[b * WINDOW : (b + 1) * WINDOW]
                        results.append((h, b, own + gate * part))
            finish(results)
            after(g)

    def products(u):
        return lax.dot_general(
            keys[u, WINDOW : WINDOW + ROWS, :HEAD],
            keys[u, :, :HEAD],
            (((1,), (1,)), ((), ())),
            preferred_element_type=F32,
        )

    def weights(scores):
        blocks = []
        none = jnp.zeros((WINDOW, WINDOW), BF16)
        for b in range(2):
            rows = scores[b * WINDOW : (b + 1) * WINDOW, b * WINDOW : (b + 3) * WINDOW]
            left = rows[:, :WINDOW] + bias[2 * b]
            mid = rows[:, WINDOW : 2 * WINDOW]
            right = rows[:, 2 * WINDOW :] + bias[2 * b + 1]
            top = jnp.max(jnp.maximum(jnp.maximum(left, right), mid), axis=1, keepdims=True)
            expo = [jnp.exp2(part - top).astype(BF16) for part in (left, mid, right)]
            blocks.append(jnp.concatenate([none] * b + expo + [none] * (1 - b), axis=1))
        return jnp.concatenate(blocks, axis=0)

    def mixed(u, expo):
        both = jnp.dot(expo, keys[u], preferred_element_type=F32)
        return both[:, :HEAD] * pl.reciprocal(both[:, HEAD:], approx=True)

    def rows_of(b):
        return pl.ds(b * WINDOW + WINDOW, WINDOW)

    for k in range(1, 8):
        mod1(k).start()
    tell(True, True)
    wait_load(LATENT)
    send_groups(LATENT, 0, 2)
    load(STALE, stale_hbm)
    keys[:, :, HEAD:] = jnp.ones((PACK, EXT, HEAD), BF16)
    query_at = lax.broadcasted_iota(jnp.int32, (WINDOW, WINDOW), 0)
    key_at = lax.broadcasted_iota(jnp.int32, (WINDOW, WINDOW), 1)
    left_bias = jnp.where(key_at >= query_at, 0.0, MASKED)
    right_bias = jnp.where(key_at <= query_at, 0.0, MASKED)
    bias[0] = jnp.where(seq == 0, MASKED, left_bias)
    bias[1] = right_bias
    bias[2] = left_bias
    bias[3] = jnp.where(seq == last, MASKED, right_bias)

    @pl.when(jnp.logical_not(inner))
    def _():
        none = pl.ds(dst_on, WINDOW)
        for arr in range(4):
            msg_in[arr, 1] = jnp.zeros((8, HEAD), F32)

            @pl.loop(0, HEADS)
            def _(h, arr=arr):
                x[arr][h, none] = jnp.zeros((WINDOW, HEAD), BF16)

    own_stats(LATENT)
    pl.semaphore_wait(from_below, 1)
    pl.semaphore_wait(from_above, 1)
    tell(True, True)
    for k in range(1, 8):
        mod1(k).wait_recv()
    joint[across] = (plane[:4] + plane[4:])[:, :4]
    for k in range(1, 4):
        mod2(k).start()
    send_groups(LATENT, 2, 4)
    wait_load(STALE)
    pl.semaphore_wait(from_below, 1)
    pl.semaphore_wait(from_above, 1)
    tell(True, False)
    own_stats(STALE)

    for k in range(1, 4):
        mod2(k).wait_recv()
    lane = lax.broadcasted_iota(jnp.int32, (8, HEAD), 1)

    def chunk(k):
        return jnp.concatenate([joint[k // 4, k % 4], jnp.zeros((4, HEAD), F32)], axis=0)

    for k in range(PLANE):
        first, second = chunk(k), chunk(k + 1)
        if k > 0:
            first = pltpu.roll(first, HEAD - 8 * k, 1)
        second = pltpu.roll(second, COLS - 8 * k, 1)
        row = jnp.where(lane < COLS - 8 * k, first, second)
        at = deep * PLANE + k
        factor = jnp.where(at < 2 * HEADS, F32(ROOT), F32(1.0 / ROOT))
        row = (row + jnp.where(at // HEADS == 1, F32(1.0), F32(0.0))) * factor
        mods[at] = row[:4]
    pl.semaphore_wait(from_below, 1)
    for k in range(1, 8):
        mod3(k).start()

    send_groups(LATENT, 4, GROUPS)
    send_groups(STALE, 0, GROUPS)
    for k in range(1, 8):
        mod3(k).wait_recv()

    def to_fresh(results):
        for h, b, value in results:
            x[FRESH][h, rows_of(b)] = value.astype(BF16)

    def to_state(results):
        now = [x[LATENT][h, rows_of(b)].astype(F32) for h, b, _ in results]
        for (h, b, value), base in zip(results, now):
            x[STATE][h, rows_of(b)] = (base + rates[0] * value).astype(BF16)

    def to_latent_out(results):
        now = [x[STATE][h, rows_of(b)].astype(F32) for h, b, _ in results]
        for (h, b, value), base in zip(results, now):
            out[0][h, b * WINDOW : (b + 1) * WINDOW] = (base + rates[1] * value).astype(BF16)

    def to_hidden_out(results):
        for h, b, value in results:
            out[1][h, b * WINDOW : (b + 1) * WINDOW] = value.astype(BF16)

    def write(which, target):
        def after(g):
            for u in range(PACK):
                h = g * PACK + u
                cols = pl.ds(pl.multiple_of(h * HEAD, HEAD), HEAD)
                pltpu.make_async_copy(out[which].at[h], target.at[:, cols], out_sem.at[which]).start()

        return after

    def early(g):
        @pl.when(g < EARLY)
        def _():
            send_halo(FRESH, g)

    halo_stats(LATENT)
    run_section(LATENT, 0, to_fresh, early)
    own_stats(FRESH)
    send_groups(FRESH, EARLY, GROUPS)
    halo_stats(STALE)
    run_section(STALE, 2, to_state, lambda g: None)
    own_stats(STATE)
    send_groups(STATE, 0, GROUPS)
    halo_stats(FRESH)
    run_section(FRESH, 3, to_latent_out, write(0, latent_out))
    halo_stats(STATE)
    run_section(STATE, 1, to_hidden_out, write(1, hidden_out))

    for which in range(2):
        pltpu.make_async_copy(out[which], out[which], out_sem.at[which]).wait()
    for k in range(1, 8):
        mod1(k).wait_send()
        mod3(k).wait_send()
    for k in range(1, 4):
        mod2(k).wait_send()
    for arr in range(4):
        for side in range(2):
            each_side(side, lambda side=side, arr=arr: message(arr, side).wait_send())
        sent = x[arr].at[:, pl.ds(0, WINDOW)]
        pltpu.make_async_copy(sent, sent, send_on.at[arr]).wait()

        @pl.when(inner)
        def _(arr=arr, sent=sent):
            pltpu.make_async_copy(sent, sent, send_off.at[arr]).wait()


def write_out(first, second, first_out, second_out, sem):
    copies = [
        pltpu.make_async_copy(first, first_out, sem.at[0]),
        pltpu.make_async_copy(second, second_out, sem.at[1]),
    ]
    for copy in copies:
        copy.start()
    for copy in copies:
        copy.wait()


def per_device(latent, stale_hidden, step_ids, sigma_table, mod_weight):
    dma = pltpu.SemaphoreType.DMA
    anywhere = pl.BlockSpec(memory_space=pl.ANY)
    fixed = pl.BlockSpec(memory_space=pltpu.HBM)
    weight = jnp.swapaxes(mod_weight, 1, 2)
    result = jax.ShapeDtypeStruct(latent.shape, latent.dtype)
    results = pl.pallas_call(
        kernel,
        out_shape=(result, result),
        in_specs=[anywhere, anywhere, fixed, fixed, fixed],
        out_specs=(anywhere, anywhere),
        scratch_shapes=[
            *[pltpu.VMEM((HEADS, EXT, HEAD), BF16)] * 4,
            *[pltpu.VMEM((HEADS, ROWS, HEAD), BF16)] * 2,
            pltpu.VMEM((4, EXT, HEAD), F32),
            pltpu.VMEM((4, EXT, HEAD), F32),
            pltpu.VMEM((4, WINDOW, WINDOW), F32),
            pltpu.VMEM((PACK, EXT, 2 * HEAD), BF16),
            pltpu.VMEM((4, 2, 8, HEAD), F32),
            pltpu.VMEM((4, 2, 8, HEAD), F32),
            pltpu.VMEM((8, 8, HEAD), F32),
            pltpu.VMEM((4, 4, 4, HEAD), F32),
            pltpu.VMEM((3 * HEADS, 4, HEAD), F32),
            dma((2,)),
            dma((2,)),
            dma((4, GROUPS)),
            dma((4, 2 * GROUPS)),
            dma((4,)),
            dma((4,)),
            dma((4, 2)),
            dma((4, 2)),
            dma((8,)),
            dma((8,)),
            dma((4,)),
            dma((4,)),
            dma((8,)),
            dma((8,)),
            pltpu.SemaphoreType.REGULAR,
            pltpu.SemaphoreType.REGULAR,
            pltpu.SMEM(step_ids.shape, jnp.int32),
            pltpu.SMEM(sigma_table.shape, jnp.int32),
            pltpu.VMEM(weight.shape, BF16),
            dma((3,)),
        ],
        compiler_params=pltpu.CompilerParams(
            collective_id=0, has_side_effects=True, vmem_limit_bytes=48 * 1024 * 1024
        ),
    )(latent, stale_hidden, *[pltpu.with_memory_space_constraint(v, pltpu.HBM) for v in (step_ids, sigma_table, weight)])
    return pl.pallas_call(
        write_out,
        out_shape=(result, result),
        in_specs=[anywhere, anywhere],
        out_specs=(fixed, fixed),
        scratch_shapes=[dma((2,))],
        compiler_params=pltpu.CompilerParams(vmem_limit_bytes=1024 * 1024),
    )(*results)


def solution(mesh):
    placed = (P("seq", None), P("seq", None), P(), P(), P("segment", None, "seq"))
    return jax.shard_map(
        per_device,
        mesh=mesh,
        in_specs=placed,
        out_specs=(P("seq", None), P("seq", None)),
        check_vma=False,
    )
```

```python
import math

import jax
import jax.numpy as jnp
from jax import lax
from jax.experimental import pallas as pl
from jax.experimental.pallas import tpu as pltpu
from jax.sharding import PartitionSpec as P

HEADS = 40
HEAD = 128
WINDOW = 128
ROWS = 256
EXT = ROWS + 2 * WINDOW
WIDTH = HEADS * HEAD
PACK = 10
GROUPS = HEADS // PACK
COLS = 120
PLANE = 15
EARLY = 2
ROOT = math.sqrt(math.log2(math.e) / HEAD)
MASKED = -1e30
MESH = pl.DeviceIdType.MESH
F32 = jnp.float32
BF16 = jnp.bfloat16

LATENT, STALE, FRESH, STATE = range(4)


def features(t_first, t_second, segment):
    shape = (8, HEAD)
    lane = lax.broadcasted_iota(jnp.int32, shape, 1).astype(F32)
    row = lax.broadcasted_iota(jnp.int32, shape, 0)
    freqs = jnp.exp(lane * (-math.log(10000.0) / HEAD))
    angles = jnp.where(row % 2 == 0, t_first, t_second) * freqs
    keep = jnp.where(row // 2 == segment, 1.0, 0.0)
    parts = []
    for value in (jnp.cos(angles), jnp.sin(angles)):
        parts.append(value / (1.0 + jnp.exp(-value)) * keep)
    return jnp.concatenate(parts, axis=1).astype(BF16)


def kernel(
    latent_hbm,
    stale_hbm,
    step_ids_hbm,
    sigma_hbm,
    weight_hbm,
    latent_out,
    hidden_out,
    x_latent,
    x_stale,
    x_fresh,
    x_state,
    out_latent,
    out_hidden,
    rstd,
    offset,
    bias,
    keys,
    msg_out,
    msg_in,
    plane,
    joint,
    mods,
    load_sem,
    out_sem,
    recv_on,
    recv_off,
    send_on,
    send_off,
    recv_msg,
    send_msg,
    recv_mod1,
    send_mod1,
    recv_mod2,
    send_mod2,
    recv_mod3,
    send_mod3,
    from_below,
    from_above,
    step_ids,
    sigma_table,
    weight,
    small_sem,
):
    x = (x_latent, x_stale, x_fresh, x_state)
    out = (out_latent, out_hidden)
    seg = lax.axis_index("segment")
    seq = lax.axis_index("seq")
    core = seq % 2
    spot = seq % 4
    across = (seq // 4) % 4
    deep = seq // 16
    quad = seg * 4 + spot
    last = 127
    on_chip = seq + 1 - 2 * core
    off_chip = (seq + 127 + 2 * core) % 128

    src_on = pl.multiple_of(256 - 128 * core, 128)
    src_off = pl.multiple_of(128 + 128 * core, 128)
    dst_on = pl.multiple_of(384 * core, 128)
    dst_off = pl.multiple_of(384 - 384 * core, 128)

    def peer_quad(k):
        other = (quad + k) % 8
        return (other // 4, seq - spot + other % 4)

    def peer_across(k):
        return (seg, seq - across * 4 + (across + k) % 4 * 4)

    def peer_deep(k):
        return (seg, (seq + 16 * k) % 128)

    def load(arr, source):
        @pl.loop(0, HEADS)
        def _(h):
            cols = pl.ds(pl.multiple_of(h * HEAD, HEAD), HEAD)
            pltpu.make_async_copy(
                source.at[:, cols], x[arr].at[h, pl.ds(WINDOW, ROWS)], load_sem.at[arr]
            ).start()

    def wait_load(arr):
        whole = x[arr].at[:, pl.ds(WINDOW, ROWS)]
        pltpu.make_async_copy(whole, whole, load_sem.at[arr]).wait()

    small = [
        pltpu.make_async_copy(source, target, small_sem.at[i])
        for i, (source, target) in enumerate(
            ((step_ids_hbm, step_ids), (sigma_hbm, sigma_table), (weight_hbm, weight))
        )
    ]
    for copy in small:
        copy.start()

    inner = (seq > 0) & (seq < last)
    above, below = peer_deep(1), peer_deep(7)
    barrier = pltpu.get_barrier_semaphore()

    @pl.when(inner)
    def _():
        for to in range(2):
            pl.semaphore_signal(barrier, inc=1, device_id=(to, off_chip), device_id_type=MESH)

    partners = [peer_quad(k) for k in range(1, 8)]
    partners += [peer_across(k) for k in range(1, 4)]
    partners += [above, below]
    for partner in partners:
        pl.semaphore_signal(barrier, inc=1, device_id=partner, device_id_type=MESH)
    load(LATENT, latent_hbm)

    for copy in small:
        copy.wait()
    times = [sigma_table[step_ids[i]].astype(F32) for i in range(3)]
    feats = features(times[0], times[1], seg)
    columns = lax.dot_general(
        feats, weight[0], (((1,), (1,)), ((), ())), preferred_element_type=F32
    )
    plane[quad] = jnp.concatenate([columns, jnp.zeros((8, HEAD - COLS), F32)], axis=1)
    rates = [(times[i + 1] - times[i]) * F32(1.0 / 1000.0) for i in range(2)]

    @pl.when(inner)
    def _():
        pl.semaphore_wait(barrier, len(partners) + 2)

    @pl.when(jnp.logical_not(inner))
    def _():
        pl.semaphore_wait(barrier, len(partners))

    def tell(up, down):
        if up:
            pl.semaphore_signal(from_below, inc=1, device_id=above, device_id_type=MESH)
        if down:
            pl.semaphore_signal(from_above, inc=1, device_id=below, device_id_type=MESH)

    def mod1(k):
        ref = plane.at[quad]
        return pltpu.make_async_remote_copy(
            ref, ref, send_mod1.at[k], recv_mod1.at[k], peer_quad(k), MESH
        )

    def mod2(k):
        ref = joint.at[across]
        return pltpu.make_async_remote_copy(
            ref, ref, send_mod2.at[k], recv_mod2.at[k], peer_across(k), MESH
        )

    def mod3(k):
        ref = mods.at[pl.ds(deep * PLANE, PLANE)]
        return pltpu.make_async_remote_copy(
            ref, ref, send_mod3.at[k], recv_mod3.at[k], peer_deep(k), MESH
        )

    def halo_on(arr, g):
        heads = pl.ds(g * PACK, PACK)
        return pltpu.make_async_remote_copy(
            x[arr].at[heads, pl.ds(src_on, WINDOW)],
            x[arr].at[heads, pl.ds(dst_on, WINDOW)],
            send_on.at[arr],
            recv_on.at[arr, g],
            (seg, on_chip),
            MESH,
        )

    def halo_off(arr, g, half, to):
        heads = pl.ds(g * PACK + half * (PACK // 2), PACK // 2)
        return pltpu.make_async_remote_copy(
            x[arr].at[heads, pl.ds(src_off, WINDOW)],
            x[arr].at[heads, pl.ds(dst_off, WINDOW)],
            send_off.at[arr],
            recv_off.at[arr, 2 * g + half],
            (to, off_chip),
            MESH,
        )

    def send_halo(arr, g):
        @pl.when(inner)
        def _():
            halo_off(arr, g, seg, 0).start()
            halo_off(arr, g, seg, 1).start()

        halo_on(arr, g).start()

    def send_groups(arr, first, end):
        @pl.loop(first, end)
        def _(g):
            send_halo(arr, g)

    def message(arr, side):
        return pltpu.make_async_remote_copy(
            msg_out.at[arr, side],
            msg_in.at[arr, side],
            send_msg.at[arr, side],
            recv_msg.at[arr, side],
            (seg, on_chip if side == 0 else off_chip),
            MESH,
        )

    def each_side(side, act):
        if side == 0:
            act()
        else:
            pl.when(inner)(act)

    def own_stats(arr):
        own = pl.ds(WINDOW, ROWS)

        def add(h, total):
            return total + x[arr][h, own].astype(F32)

        total = lax.fori_loop(0, HEADS, add, jnp.zeros((ROWS, HEAD), F32), unroll=4)
        mean = jnp.sum(total, axis=1, keepdims=True) * F32(1.0 / WIDTH)
        mean = jnp.broadcast_to(mean, (ROWS, HEAD))
        offset[arr, own] = mean

        def add_square(h, total):
            part = x[arr][h, own].astype(F32) - offset[arr, own]
            return total + part * part

        total = lax.fori_loop(0, HEADS, add_square, jnp.zeros((ROWS, HEAD), F32), unroll=4)
        var = jnp.sum(total, axis=1, keepdims=True) * F32(1.0 / WIDTH)
        scale = jnp.broadcast_to(lax.rsqrt(var + 1e-06), (ROWS, HEAD))
        rstd[arr, own] = scale
        offset[arr, own] = -mean * scale
        row = lax.broadcasted_iota(jnp.int32, (8, HEAD), 0)
        for side, start in ((0, src_on), (1, src_off)):
            first = rstd[arr, pl.ds(start, WINDOW)].T[:8]
            second = offset[arr, pl.ds(start, WINDOW)].T[:8]
            msg_out[arr, side] = jnp.where(row == 0, first, second)
            each_side(side, lambda side=side: message(arr, side).start())

    def halo_stats(arr):
        for side, start in ((0, dst_off), (1, dst_on)):
            each_side(side, lambda side=side: message(arr, side).wait_recv())
            rows = pl.ds(start, WINDOW)
            got = msg_in[arr, side]
            rstd[arr, rows] = jnp.broadcast_to(got[0:1], (WINDOW, HEAD)).T
            offset[arr, rows] = jnp.broadcast_to(got[1:2], (WINDOW, HEAD)).T

    def run_section(arr, mod_row, finish, after):
        @pl.loop(0, GROUPS)
        def _(g):
            halo_on(arr, g).wait_recv()

            @pl.when(inner)
            def _():
                halo_off(arr, g, 0, seg).wait_recv()
                halo_off(arr, g, 1, seg).wait_recv()

            heads = [g * PACK + u for u in range(PACK)]
            for u, h in enumerate(heads):
                shift = mods[h][mod_row : mod_row + 1]
                scale = mods[HEADS + h][mod_row : mod_row + 1]
                raw = x[arr][h].astype(F32)
                normed = (raw * rstd[arr] + offset[arr]) * scale + shift
                keys[u, :, :HEAD] = normed.astype(BF16)
            results = []
            scores, expo = {}, {}
            for step in range(PACK + 2):
                if step < PACK:
                    scores[step] = products(step)
                if 1 <= step <= PACK:
                    expo[step - 1] = weights(scores.pop(step - 1))
                if step >= 2:
                    u = step - 2
                    h = heads[u]
                    gate = mods[2 * HEADS + h][mod_row : mod_row + 1]
                    attn = mixed(u, expo.pop(u))
                    for b in range(2):
                        own = x[arr][h, rows_of(b)].astype(F32)
                        part = attn[b * WINDOW : (b + 1) * WINDOW]
                        results.append((h, b, own + gate * part))
            finish(results)
            after(g)

    def products(u):
        return lax.dot_general(
            keys[u, WINDOW : WINDOW + ROWS, :HEAD],
            keys[u, :, :HEAD],
            (((1,), (1,)), ((), ())),
            preferred_element_type=F32,
        )

    def weights(scores):
        blocks = []
        none = jnp.zeros((WINDOW, WINDOW), BF16)
        for b in range(2):
            rows = scores[b * WINDOW : (b + 1) * WINDOW, b * WINDOW : (b + 3) * WINDOW]
            left = rows[:, :WINDOW] + bias[2 * b]
            mid = rows[:, WINDOW : 2 * WINDOW]
            right = rows[:, 2 * WINDOW :] + bias[2 * b + 1]
            top = jnp.max(jnp.maximum(jnp.maximum(left, right), mid), axis=1, keepdims=True)
            expo = [jnp.exp2(part - top).astype(BF16) for part in (left, mid, right)]
            blocks.append(jnp.concatenate([none] * b + expo + [none] * (1 - b), axis=1))
        return jnp.concatenate(blocks, axis=0)

    def mixed(u, expo):
        both = jnp.dot(expo, keys[u], preferred_element_type=F32)
        return both[:, :HEAD] * pl.reciprocal(both[:, HEAD:], approx=True)

    def rows_of(b):
        return pl.ds(b * WINDOW + WINDOW, WINDOW)

    for k in range(1, 8):
        mod1(k).start()
    tell(True, True)
    wait_load(LATENT)
    send_groups(LATENT, 0, 2)
    load(STALE, stale_hbm)
    keys[:, :, HEAD:] = jnp.ones((PACK, EXT, HEAD), BF16)
    query_at = lax.broadcasted_iota(jnp.int32, (WINDOW, WINDOW), 0)
    key_at = lax.broadcasted_iota(jnp.int32, (WINDOW, WINDOW), 1)
    left_bias = jnp.where(key_at >= query_at, 0.0, MASKED)
    right_bias = jnp.where(key_at <= query_at, 0.0, MASKED)
    bias[0] = jnp.where(seq == 0, MASKED, left_bias)
    bias[1] = right_bias
    bias[2] = left_bias
    bias[3] = jnp.where(seq == last, MASKED, right_bias)

    @pl.when(jnp.logical_not(inner))
    def _():
        none = pl.ds(dst_on, WINDOW)
        for arr in range(4):
            msg_in[arr, 1] = jnp.zeros((8, HEAD), F32)

            @pl.loop(0, HEADS)
            def _(h, arr=arr):
                x[arr][h, none] = jnp.zeros((WINDOW, HEAD), BF16)

    own_stats(LATENT)
    pl.semaphore_wait(from_below, 1)
    pl.semaphore_wait(from_above, 1)
    tell(True, True)
    for k in range(1, 8):
        mod1(k).wait_recv()
    joint[across] = (plane[:4] + plane[4:])[:, :4]
    for k in range(1, 4):
        mod2(k).start()
    send_groups(LATENT, 2, 3)
    wait_load(STALE)
    pl.semaphore_wait(from_below, 1)
    pl.semaphore_wait(from_above, 1)
    tell(True, False)

    for k in range(1, 4):
        mod2(k).wait_recv()
    lane = lax.broadcasted_iota(jnp.int32, (8, HEAD), 1)

    def chunk(k):
        return jnp.concatenate([joint[k // 4, k % 4], jnp.zeros((4, HEAD), F32)], axis=0)

    for k in range(PLANE):
        first, second = chunk(k), chunk(k + 1)
        if k > 0:
            first = pltpu.roll(first, HEAD - 8 * k, 1)
        second = pltpu.roll(second, COLS - 8 * k, 1)
        row = jnp.where(lane < COLS - 8 * k, first, second)
        at = deep * PLANE + k
        factor = jnp.where(at < 2 * HEADS, F32(ROOT), F32(1.0 / ROOT))
        row = (row + jnp.where(at // HEADS == 1, F32(1.0), F32(0.0))) * factor
        mods[at] = row[:4]
    pl.semaphore_wait(from_below, 1)
    for k in range(1, 8):
        mod3(k).start()

    send_groups(LATENT, 3, GROUPS)
    send_groups(STALE, 0, GROUPS)
    own_stats(STALE)
    for k in range(1, 8):
        mod3(k).wait_recv()

    def to_fresh(results):
        for h, b, value in results:
            x[FRESH][h, rows_of(b)] = value.astype(BF16)

    def to_state(results):
        now = [x[LATENT][h, rows_of(b)].astype(F32) for h, b, _ in results]
        for (h, b, value), base in zip(results, now):
            x[STATE][h, rows_of(b)] = (base + rates[0] * value).astype(BF16)

    def to_latent_out(results):
        now = [x[STATE][h, rows_of(b)].astype(F32) for h, b, _ in results]
        for (h, b, value), base in zip(results, now):
            out[0][h, b * WINDOW : (b + 1) * WINDOW] = (base + rates[1] * value).astype(BF16)

    def to_hidden_out(results):
        for h, b, value in results:
            out[1][h, b * WINDOW : (b + 1) * WINDOW] = value.astype(BF16)

    def write(which, target):
        def after(g):
            for u in range(PACK):
                h = g * PACK + u
                cols = pl.ds(pl.multiple_of(h * HEAD, HEAD), HEAD)
                pltpu.make_async_copy(out[which].at[h], target.at[:, cols], out_sem.at[which]).start()

        return after

    def early(g):
        @pl.when(g < EARLY)
        def _():
            send_halo(FRESH, g)

    halo_stats(LATENT)
    run_section(LATENT, 0, to_fresh, early)
    own_stats(FRESH)
    send_groups(FRESH, EARLY, GROUPS)
    halo_stats(STALE)
    run_section(STALE, 2, to_state, lambda g: None)
    own_stats(STATE)
    send_groups(STATE, 0, GROUPS)
    halo_stats(FRESH)
    run_section(FRESH, 3, to_latent_out, write(0, latent_out))
    halo_stats(STATE)
    run_section(STATE, 1, to_hidden_out, write(1, hidden_out))

    for which in range(2):
        pltpu.make_async_copy(out[which], out[which], out_sem.at[which]).wait()
    for k in range(1, 8):
        mod1(k).wait_send()
        mod3(k).wait_send()
    for k in range(1, 4):
        mod2(k).wait_send()
    for arr in range(4):
        for side in range(2):
            each_side(side, lambda side=side, arr=arr: message(arr, side).wait_send())
        sent = x[arr].at[:, pl.ds(0, WINDOW)]
        pltpu.make_async_copy(sent, sent, send_on.at[arr]).wait()

        @pl.when(inner)
        def _(arr=arr, sent=sent):
            pltpu.make_async_copy(sent, sent, send_off.at[arr]).wait()


def write_out(first, second, first_out, second_out, sem):
    copies = [
        pltpu.make_async_copy(first, first_out, sem.at[0]),
        pltpu.make_async_copy(second, second_out, sem.at[1]),
    ]
    for copy in copies:
        copy.start()
    for copy in copies:
        copy.wait()


def per_device(latent, stale_hidden, step_ids, sigma_table, mod_weight):
    dma = pltpu.SemaphoreType.DMA
    anywhere = pl.BlockSpec(memory_space=pl.ANY)
    fixed = pl.BlockSpec(memory_space=pltpu.HBM)
    weight = jnp.swapaxes(mod_weight, 1, 2)
    result = jax.ShapeDtypeStruct(latent.shape, latent.dtype)
    results = pl.pallas_call(
        kernel,
        out_shape=(result, result),
        in_specs=[anywhere, anywhere, fixed, fixed, fixed],
        out_specs=(anywhere, anywhere),
        scratch_shapes=[
            *[pltpu.VMEM((HEADS, EXT, HEAD), BF16)] * 4,
            *[pltpu.VMEM((HEADS, ROWS, HEAD), BF16)] * 2,
            pltpu.VMEM((4, EXT, HEAD), F32),
            pltpu.VMEM((4, EXT, HEAD), F32),
            pltpu.VMEM((4, WINDOW, WINDOW), F32),
            pltpu.VMEM((PACK, EXT, 2 * HEAD), BF16),
            pltpu.VMEM((4, 2, 8, HEAD), F32),
            pltpu.VMEM((4, 2, 8, HEAD), F32),
            pltpu.VMEM((8, 8, HEAD), F32),
            pltpu.VMEM((4, 4, 4, HEAD), F32),
            pltpu.VMEM((3 * HEADS, 4, HEAD), F32),
            dma((2,)),
            dma((2,)),
            dma((4, GROUPS)),
            dma((4, 2 * GROUPS)),
            dma((4,)),
            dma((4,)),
            dma((4, 2)),
            dma((4, 2)),
            dma((8,)),
            dma((8,)),
            dma((4,)),
            dma((4,)),
            dma((8,)),
            dma((8,)),
            pltpu.SemaphoreType.REGULAR,
            pltpu.SemaphoreType.REGULAR,
            pltpu.SMEM(step_ids.shape, jnp.int32),
            pltpu.SMEM(sigma_table.shape, jnp.int32),
            pltpu.VMEM(weight.shape, BF16),
            dma((3,)),
        ],
        compiler_params=pltpu.CompilerParams(
            collective_id=0, has_side_effects=True, vmem_limit_bytes=48 * 1024 * 1024
        ),
    )(latent, stale_hidden, *[pltpu.with_memory_space_constraint(v, pltpu.HBM) for v in (step_ids, sigma_table, weight)])
    return pl.pallas_call(
        write_out,
        out_shape=(result, result),
        in_specs=[anywhere, anywhere],
        out_specs=(fixed, fixed),
        scratch_shapes=[dma((2,))],
        compiler_params=pltpu.CompilerParams(vmem_limit_bytes=1024 * 1024),
    )(*results)


def solution(mesh):
    placed = (P("seq", None), P("seq", None), P(), P(), P("segment", None, "seq"))
    return jax.shard_map(
        per_device,
        mesh=mesh,
        in_specs=placed,
        out_specs=(P("seq", None), P("seq", None)),
        check_vma=False,
    )
```
